32 devices in a mesh: grp: 1, blk: 32 (over z, y, x, core).
Axes of the slice: x: 2, y: 2, z: 4, core: 2. Of those that a mesh axis runs over, the one named last changes fastest.
Arguments:
- grad_out: bfloat16 [128, 1440, 384], P(('grp', 'blk')), may hold values from -6 to 6
- coef_saved: bfloat16 [2, 256, 513, 384], P(None, ('grp', 'blk')), may hold values from -0.0546875 to 0.0546875
- mixing: bfloat16 [384, 384], replicated, may hold values from -0.3125 to 0.3125
- order_pairs: int32 [256], replicated, may hold values from 0 to 255, each once
Outputs:
- grad_in: bfloat16 [128, 1440, 384], P(('grp', 'blk'))
- weight_grad: float32 [384, 384], P(('grp', 'blk'))
The draws below stay inside these ranges and needn't reach their ends.
Inputs may be any that keep to these rules, and one draw needn't show every extreme that they name: Each pair appears once; position q holds the orders order_pairs[q] and 511 - order_pairs[q]; the device with index i along blk holds positions i * 8 to (i + 1) * 8 - 1 of coef_saved.
All inputs are finite; a program needn't handle non-finite values.
Results may differ from the reference program's by a relative error of at most 0.008.
Values may be sent and summed in bfloat16 or wider, within the bound.
A program may use at most 128 MiB of HBM per device.

```python
import math
import jax
import jax.numpy as jnp
from jax import lax

C = 384
NLON = 1440
L = 512
NLAT = 128
PAIRS = 256


def spiked(result, stream_key, source, target, parts, factor):
    def block_of(dim):
        return (jnp.arange(result.shape[dim]) // (result.shape[dim] // parts)).reshape((-1,) + (1,) * (result.ndim - 1 - dim))

    first = jax.random.permutation(stream_key, parts)[block_of(target)]
    second = (block_of(target) + parts // 2) % parts
    return jnp.where((block_of(source) == first) | (block_of(source) == second), factor * result, result)


def steps_of(stream_key, shape, shards, low, top_value):
    gain, own = 1.0, jax.random.fold_in(stream_key, 6)
    for axis_at, shards_of in shards:
        steps = jnp.exp(jax.random.uniform(jax.random.fold_in(own, axis_at), (shards_of,), jnp.float32, low / len(shards), top_value / len(shards)))
        gain = gain * jnp.repeat(steps, shape[axis_at] // shards_of).reshape([-1 if axis == axis_at else 1 for axis in range(len(shape))])
    return gain


def normal_values(stream_key, shape, scale, reach, split=(), kind=jnp.bfloat16):
    loudness = steps_of(stream_key, shape, split, -0.22, 0.18) if split else 1.0
    array = jax.random.normal(stream_key, shape, jnp.float32) * scale * loudness
    return jnp.minimum(jnp.maximum(array, -reach), reach).astype(kind)


def bell_draw_with(rng, dims, scale, bound, pieces, heavy, held_as=jnp.bfloat16):
    array = scale * jax.random.normal(rng, dims, jnp.float32)
    if pieces:
        array = array * steps_of(rng, dims, pieces, -0.22, 0.18)
    return jnp.clip(spiked(array, jax.random.fold_in(rng, 3), *heavy), -bound, bound).astype(held_as)


def setup_inputs(seed: int = 0, part: int = 0) -> dict:
    splits = jax.random.split(jax.random.key(seed), 5)
    part_keys = jax.random.split(jax.random.fold_in(splits[4], part), 5)
    return {
        "grad_out": normal_values(part_keys[0], (NLAT, NLON, C), 1.0, 6.0, ((0, 32),)),
        "coef_saved": bell_draw_with(part_keys[1], (2, PAIRS, L + 1, C), (1 / (2 * PAIRS * (L + 1)) ** 0.5), 0.0546875, ((1, 32),), (1, 3, 32, 2.75)),
        "mixing": normal_values(splits[2], (C, C), C ** -0.5, 0.3125),
        "order_pairs": jax.random.permutation(splits[3], PAIRS).astype(jnp.int32),
    }


def longitude_table(order_pairs, degrees, points):
    slot_orders = jnp.stack([order_pairs, degrees - 1 - order_pairs], axis=1).reshape(-1).astype(jnp.int32)
    products = slot_orders[:, None] * jnp.arange(points, dtype=jnp.int32)[None, :] % points
    angles = 2.0 * math.pi / points * products.astype(jnp.float32)
    norm_factor = 1.0 / math.sqrt(points)
    return jnp.concatenate([jnp.cos(angles) * norm_factor, -jnp.sin(angles) * norm_factor], axis=0).astype(jnp.bfloat16)

def legendre_rows(pair_ids, cycle_total, degrees, unrolled):
    colatitude = math.pi * (jnp.arange(cycle_total, dtype=jnp.float32) + 0.5) / cycle_total
    cosine_rows = jnp.cos(colatitude)[None, :]
    sine_rows = jnp.sin(colatitude)[None, :]
    first_order = pair_ids.astype(jnp.float32)[:, None]
    second_order = degrees - 1.0 - first_order
    boundary = degrees - first_order
    rescale_limit = 4294967296.0
    rescale_factor = 1.0 / 4294967296.0
    rescale_log = 32.0 * math.log(2.0)

    def start_log(order_value):
        return 0.5 * (jnp.log((2.0 * order_value + 1.0) / (4.0 * math.pi)) + lax.lgamma(order_value + 0.5) - lax.lgamma(order_value + 1.0) - 0.5 * math.log(math.pi)) + order_value * jnp.log(sine_rows)
    first_start = start_log(first_order)
    second_start = start_log(second_order)

    def advance(state_triple, row_index):
        previous, earlier, offset = state_triple
        position = row_index.astype(jnp.float32)
        in_first = position < boundary
        harmonic = jnp.where(in_first, first_order, second_order)
        degree = jnp.where(in_first, first_order + position, second_order + position - boundary)
        degree_below = degree - 1.0
        factor_a = jnp.sqrt(jnp.maximum(4.0 * degree * degree - 1.0, 1.0) / jnp.maximum(degree * degree - harmonic * harmonic, 1.0))
        factor_b = jnp.sqrt(jnp.maximum(degree_below * degree_below - harmonic * harmonic, 0.0) / jnp.maximum(4.0 * degree_below * degree_below - 1.0, 1.0))
        recurred = factor_a * (cosine_rows * previous - factor_b * earlier)
        restart = degree == harmonic
        recurred = jnp.where(restart, jnp.ones_like(recurred), recurred)
        offset = jnp.where(restart, jnp.where(in_first, first_start, second_start), offset)
        emitted = recurred * jnp.exp(offset)
        too_big = jnp.abs(recurred) > rescale_limit
        next_prev = jnp.where(too_big, recurred * rescale_factor, recurred)
        next_earlier = jnp.where(too_big, previous * rescale_factor, previous)
        next_offset = jnp.where(too_big, offset + rescale_log, offset)
        return ((next_prev, next_earlier, next_offset), emitted)
    empty_rows = jnp.zeros((pair_ids.shape[0], cycle_total), jnp.float32)
    final_state, row_values = lax.scan(advance, (empty_rows, empty_rows, empty_rows), jnp.arange(degrees + 1, dtype=jnp.int32), unroll=unrolled)
    legendre_values = jnp.transpose(row_values, (1, 0, 2))
    table_scale = math.sqrt(2.0 * math.pi * math.pi / cycle_total)
    synth_table = (legendre_values * table_scale).astype(jnp.bfloat16)
    anal_table = (legendre_values * (table_scale * sine_rows)).astype(jnp.bfloat16)
    return (synth_table, anal_table, boundary)

def reference(grad_out, coef_saved, mixing, order_pairs):
    lon_table = longitude_table(order_pairs, L, NLON)
    spectral = jnp.einsum('sn,jnc->jsc', lon_table.astype(jnp.float32), grad_out.astype(jnp.float32)).astype(jnp.bfloat16)
    synth_table, anal_table, boundary = legendre_rows(order_pairs, NLAT, L, 1)
    in_first = (jnp.arange(L + 1, dtype=jnp.float32)[None, :] < boundary)[None, :, :, None]
    grouped = spectral.reshape(NLAT, 2, PAIRS, 2, C).astype(jnp.float32)
    both_parts = jnp.einsum('qkj,jrqtc->trqkc', synth_table.astype(jnp.float32), grouped)
    coef_grad = jnp.where(in_first, both_parts[0], both_parts[1]).astype(jnp.bfloat16)
    weight_grad = jnp.einsum('rqkc,rqkd->cd', coef_saved.astype(jnp.float32), coef_grad.astype(jnp.float32))
    mixed_grad = jnp.einsum('rqkd,cd->rqkc', coef_grad.astype(jnp.float32), mixing.astype(jnp.float32)).astype(jnp.bfloat16)
    empty_part = jnp.zeros_like(mixed_grad)
    order_split = jnp.stack([jnp.where(in_first, mixed_grad, empty_part), jnp.where(in_first, empty_part, mixed_grad)])
    cycle_grad = jnp.einsum('qkj,trqkc->jrqtc', anal_table.astype(jnp.float32), order_split.astype(jnp.float32)).astype(jnp.bfloat16)
    cycle_grad = cycle_grad.reshape(NLAT, 2 * L, C)
    grad_in = jnp.einsum('sn,jsc->jnc', lon_table.astype(jnp.float32), cycle_grad.astype(jnp.float32)).astype(jnp.bfloat16)
    return (grad_in, weight_grad)
```

```python
import functools
import math

import jax
import jax.numpy as jnp
from jax import lax
from jax.experimental import pallas as pl
from jax.experimental.pallas import tpu as pltpu
from jax.sharding import PartitionSpec as P

LANES = 128
VMEM_LIMIT = 48 * 1024 * 1024


def compiler_params(dims=1):
    return pltpu.CompilerParams(
        vmem_limit_bytes=VMEM_LIMIT, dimension_semantics=("arbitrary",) * dims
    )


def cost(flops, moved):
    return pl.CostEstimate(flops=int(flops), bytes_accessed=int(moved), transcendentals=0)


def angle_parts(slot_orders, points):
    devices, slots = slot_orders.shape
    blocks = -(-points // LANES)

    def angles(multiples):
        products = slot_orders[:, :, None] * multiples % points
        return 2.0 * math.pi / points * products.astype(jnp.float32)

    coarse = angles(LANES * jnp.arange(blocks, dtype=jnp.int32))
    fine = angles(jnp.arange(LANES, dtype=jnp.int32))
    norm_factor = 1.0 / math.sqrt(points)
    fine_cos = jnp.cos(fine) * norm_factor
    fine_sin = jnp.sin(fine) * norm_factor
    rows = devices * 2 * slots

    def rows_of(first, second):
        return jnp.stack([first, second], axis=1).reshape(rows, -1)

    coarse_cos, coarse_sin = jnp.cos(coarse), jnp.sin(coarse)
    return (
        rows_of(coarse_cos, coarse_cos),
        rows_of(coarse_sin, coarse_sin),
        rows_of(fine_cos, -fine_sin),
        rows_of(fine_sin, fine_cos),
    )


def spectrum_kernel(points, ca_ref, sa_ref, cb_ref, sb_ref, grid_ref, out_ref, table):
    @pl.when(pl.program_id(0) == 0)
    def _():
        for start in range(0, points, LANES):
            width = min(LANES, points - start)
            at = start // LANES
            part = (
                ca_ref[:, at : at + 1] * cb_ref[:, :width]
                - sa_ref[:, at : at + 1] * sb_ref[:, :width]
            )
            table[:, start : start + width] = part.astype(jnp.bfloat16)

    result = jnp.dot(table[...], grid_ref[0], preferred_element_type=jnp.float32)
    devices, _, rows, channels = out_ref.shape
    out_ref[:, 0] = result.reshape(devices, rows, channels).astype(jnp.bfloat16)


def spectrum(parts, grad_out, devices):
    cycles, points, channels = grad_out.shape
    total = parts[0].shape[0]
    rows = total // devices

    def whole(array):
        return pl.BlockSpec(array.shape, lambda j: (0, 0))

    return pl.pallas_call(
        functools.partial(spectrum_kernel, points),
        grid=(cycles,),
        in_specs=[whole(part) for part in parts]
        + [pl.BlockSpec((1, points, channels), lambda j: (j, 0, 0))],
        out_specs=pl.BlockSpec((devices, 1, rows, channels), lambda j: (0, j, 0, 0)),
        out_shape=jax.ShapeDtypeStruct((devices, cycles, rows, channels), jnp.bfloat16),
        scratch_shapes=[pltpu.VMEM((total, points), jnp.bfloat16)],
        compiler_params=compiler_params(),
        cost_estimate=cost(
            2 * cycles * total * points * channels, 2 * cycles * channels * (points + total)
        ),
    )(*parts, grad_out)


def grid_kernel(points, chunks, *refs):
    tables = refs[: 4 * chunks]
    received = refs[4 * chunks : 5 * chunks]
    out_ref = refs[5 * chunks]
    scratch = refs[5 * chunks + 1 :]

    @pl.when(pl.program_id(0) == 0)
    def _():
        for h in range(chunks):
            ca_ref, sa_ref, cb_ref, sb_ref = tables[4 * h : 4 * h + 4]
            for start in range(0, points, LANES):
                width = min(LANES, points - start)
                at = start // LANES
                part = (
                    ca_ref[at : at + 1, :] * cb_ref[:width, :]
                    - sa_ref[at : at + 1, :] * sb_ref[:width, :]
                )
                scratch[h][start : start + width, :] = part.astype(jnp.bfloat16)

    total = None
    for h in range(chunks):
        devices, _, rows, channels = received[h].shape
        block = received[h][:, 0].reshape(devices * rows, channels)
        term = jnp.dot(scratch[h][...], block, preferred_element_type=jnp.float32)
        total = term if total is None else total + term
    out_ref[0] = total.astype(jnp.bfloat16)


def grid_sum(parts_list, received, points):
    chunks = len(received)
    devices, cycles, rows, channels = received[0].shape
    total = devices * rows
    tables = [part.T for parts in parts_list for part in parts]
    return pl.pallas_call(
        functools.partial(grid_kernel, points, chunks),
        grid=(cycles,),
        in_specs=[pl.BlockSpec(t.shape, lambda j: (0, 0)) for t in tables]
        + [pl.BlockSpec((devices, 1, rows, channels), lambda j: (0, j, 0, 0))] * chunks,
        out_specs=pl.BlockSpec((1, points, channels), lambda j: (j, 0, 0)),
        out_shape=jax.ShapeDtypeStruct((cycles, points, channels), jnp.bfloat16),
        scratch_shapes=[pltpu.VMEM((points, total), jnp.bfloat16)] * chunks,
        compiler_params=compiler_params(),
        cost_estimate=cost(
            2 * cycles * total * points * channels * chunks,
            2 * cycles * channels * (points + total * chunks),
        ),
    )(*tables, *received)


def legendre_kernel(
    pairs, degrees, scale, order_ref, cos_ref, sin_ref, start1_ref, start2_ref,
    synth_ref, anal_ref, values,
):
    group = order_ref.shape[0]
    first_order = order_ref[...]
    second_order = degrees - 1.0 - first_order
    boundary = degrees - first_order
    cosine = cos_ref[...]
    first_start = start1_ref[...]
    second_start = start2_ref[...]
    limit = 4294967296.0
    factor = 1.0 / 4294967296.0
    rescale_log = 32.0 * math.log(2.0)
    rows = degrees + 1

    def advance(row, state):
        previous, earlier, offset = state
        position = jnp.full(first_order.shape, row, jnp.int32).astype(jnp.float32)
        in_first = position < boundary
        harmonic = jnp.where(in_first, first_order, second_order)
        degree = jnp.where(in_first, first_order + position, second_order + position - boundary)
        below = degree - 1.0
        square = harmonic * harmonic
        factor_a = jnp.sqrt(
            jnp.maximum(4.0 * degree * degree - 1.0, 1.0)
            / jnp.maximum(degree * degree - square, 1.0)
        )
        factor_b = jnp.sqrt(
            jnp.maximum(below * below - square, 0.0) / jnp.maximum(4.0 * below * below - 1.0, 1.0)
        )
        restart = degree == harmonic
        recurred = factor_a * (cosine * previous - factor_b * earlier)
        recurred = jnp.where(restart, 1.0, recurred)
        offset = jnp.where(restart, jnp.where(in_first, first_start, second_start), offset)
        values[pl.ds(pl.multiple_of(row * group, group), group), :] = recurred * jnp.exp(offset)
        too_big = jnp.abs(recurred) > limit
        return (
            jnp.where(too_big, recurred * factor, recurred),
            jnp.where(too_big, previous * factor, previous),
            jnp.where(too_big, offset + rescale_log, offset),
        )

    empty = jnp.zeros(first_order.shape, jnp.float32)
    steps = 9
    while rows % steps:
        steps -= 1

    def several(at, state):
        for i in range(steps):
            state = advance(at * steps + i, state)
        return state

    lax.fori_loop(0, rows // steps, several, (empty, empty, empty))

    for q in range(pairs):
        block = values[pl.ds(q, rows, stride=group), :]
        row_index = lax.broadcasted_iota(jnp.int32, block.shape, 0).astype(jnp.float32)
        in_first = row_index < boundary[q : q + 1, :]
        sine = sin_ref[q : q + 1, :]
        for ref, weights in ((synth_ref, scale), (anal_ref, scale * sine)):
            scaled = block * weights
            ref[q, :, :LANES] = jnp.where(in_first, scaled, 0.0).astype(jnp.bfloat16)
            ref[q, :, LANES:] = jnp.where(in_first, 0.0, scaled).astype(jnp.bfloat16)


def legendre_tables(pair_ids, cycle_total, degrees):
    pairs = pair_ids.shape[0]
    group = -(-pairs // 8) * 8
    padded = jnp.concatenate([pair_ids, jnp.zeros((group - pairs,), pair_ids.dtype)])
    colatitude = math.pi * (jnp.arange(cycle_total, dtype=jnp.float32) + 0.5) / cycle_total
    cosine_rows = jnp.cos(colatitude)[None, :]
    sine_rows = jnp.sin(colatitude)[None, :]
    first_order = padded.astype(jnp.float32)[:, None]
    second_order = degrees - 1.0 - first_order

    def start_log(order_value):
        return 0.5 * (
            jnp.log((2.0 * order_value + 1.0) / (4.0 * math.pi))
            + lax.lgamma(order_value + 0.5)
            - lax.lgamma(order_value + 1.0)
            - 0.5 * math.log(math.pi)
        ) + order_value * jnp.log(sine_rows)

    shape = (group, cycle_total)
    operands = [
        jnp.broadcast_to(value, shape)
        for value in (
            first_order, cosine_rows, sine_rows, start_log(first_order), start_log(second_order),
        )
    ]
    rows = degrees + 1
    table = jax.ShapeDtypeStruct((pairs, rows, 2 * cycle_total), jnp.bfloat16)
    return pl.pallas_call(
        functools.partial(
            legendre_kernel, pairs, degrees, math.sqrt(2.0 * math.pi * math.pi / cycle_total)
        ),
        grid=(cycle_total // LANES,),
        in_specs=[pl.BlockSpec((group, LANES), lambda i: (0, i))] * 5,
        out_specs=[pl.BlockSpec((pairs, rows, 2 * LANES), lambda i: (0, 0, i))] * 2,
        out_shape=[table, table],
        scratch_shapes=[pltpu.VMEM((rows * group, LANES), jnp.float32)],
        compiler_params=compiler_params(),
        cost_estimate=cost(2e10, 8 * pairs * rows * cycle_total),
    )(*operands)


def mix_kernel(synth_ref, anal_ref, grouped_ref, saved_ref, mixing_ref, cycle_ref, weight_ref):
    @pl.when(pl.program_id(0) == 0)
    def _():
        weight_ref[...] = jnp.zeros_like(weight_ref)

    channels = mixing_ref.shape[0]
    contract_first = (((0,), (0,)), ((), ()))
    contract_last = (((1,), (1,)), ((), ()))
    coef = jnp.dot(
        synth_ref[0], grouped_ref[0], preferred_element_type=jnp.float32
    ).astype(jnp.bfloat16)
    for r in range(2):
        part = coef[:, r * channels : (r + 1) * channels]
        weight_ref[...] += lax.dot_general(
            saved_ref[r, 0], part, contract_first, preferred_element_type=jnp.float32
        )
        mixed = lax.dot_general(
            part, mixing_ref[...], contract_last, preferred_element_type=jnp.float32
        ).astype(jnp.bfloat16)
        cycle_ref[0, :, r * channels : (r + 1) * channels] = lax.dot_general(
            anal_ref[0], mixed, contract_first, preferred_element_type=jnp.float32
        ).astype(jnp.bfloat16)


def mix(synth, anal, grouped, saved, mixing, first):
    count, depth, width = grouped.shape
    rows, channels = saved.shape[2:]
    return pl.pallas_call(
        mix_kernel,
        grid=(count,),
        in_specs=[
            pl.BlockSpec((1, rows, depth), lambda q: (q + first, 0, 0)),
            pl.BlockSpec((1, rows, depth), lambda q: (q + first, 0, 0)),
            pl.BlockSpec((1, depth, width), lambda q: (q, 0, 0)),
            pl.BlockSpec((2, 1, rows, channels), lambda q: (0, q + first, 0, 0)),
            pl.BlockSpec((channels, channels), lambda q: (0, 0)),
        ],
        out_specs=[
            pl.BlockSpec((1, depth, width), lambda q: (q, 0, 0)),
            pl.BlockSpec((channels, channels), lambda q: (0, 0)),
        ],
        out_shape=[
            jax.ShapeDtypeStruct((count, depth, width), jnp.bfloat16),
            jax.ShapeDtypeStruct((channels, channels), jnp.float32),
        ],
        compiler_params=compiler_params(),
        cost_estimate=cost(
            4 * count * rows * width * (depth + channels), 4 * count * (depth + rows) * width
        ),
    )(synth, anal, grouped, saved, mixing)


def per_device(grad_out, coef_saved, mixing, order_pairs):
    devices = lax.axis_size("blk")
    own_index = lax.axis_index("blk")
    cycle_count, points, channels = grad_out.shape
    cycle_total = cycle_count * devices
    groups = cycle_total // LANES
    pair_count = coef_saved.shape[1]
    degrees = coef_saved.shape[2] - 1
    chunks = 2 if pair_count % 8 == 0 else 1
    size = pair_count // chunks

    by_owner = order_pairs.reshape(devices, pair_count)
    slot_orders = jnp.stack([by_owner, degrees - 1 - by_owner], axis=2)
    parts_list = []
    for h in range(chunks):
        slots = slot_orders[:, h * size : (h + 1) * size].reshape(devices, 2 * size)
        parts_list.append(angle_parts(slots, points))

    exchange = functools.partial(
        lax.all_to_all, axis_name="blk", split_axis=0, concat_axis=0, tiled=True
    )
    own_pairs = lax.dynamic_slice_in_dim(order_pairs, own_index * pair_count, pair_count)
    spectra = []
    for h in range(chunks):
        spectra.append(spectrum(parts_list[h], grad_out, devices))
        if h + 1 < chunks:
            spectra[h], grad_out = lax.optimization_barrier((spectra[h], grad_out))
    own_pairs, spectra[-1] = lax.optimization_barrier((own_pairs, spectra[-1]))
    received = [exchange(s) for s in spectra]
    synth, anal = legendre_tables(own_pairs, cycle_total, degrees)

    returned, weight = [], None
    for h in range(chunks):
        grouped = received[h].reshape(groups, LANES, 2, size, 2, channels)
        grouped = jnp.transpose(grouped, (3, 0, 4, 1, 2, 5))
        grouped = grouped.reshape(size, 2 * cycle_total, 2 * channels)
        cycle_part, share = mix(synth, anal, grouped, coef_saved, mixing, h * size)
        weight = share if weight is None else weight + share
        cycle_part = cycle_part.reshape(size, groups, 2, LANES, 2, channels)
        cycle_part = jnp.transpose(cycle_part, (1, 3, 4, 0, 2, 5))
        returned.append(exchange(cycle_part.reshape(devices, cycle_count, 4 * size, channels)))
    shares = exchange(weight.reshape(devices, channels // devices, channels))
    weight_grad = jnp.sum(shares, axis=0)
    grad_in = grid_sum(parts_list, returned, points)
    return (grad_in, weight_grad)


def solution(mesh):
    return jax.shard_map(
        per_device,
        mesh=mesh,
        in_specs=(P(("grp", "blk"), None, None), P(None, ("grp", "blk"), None, None), P(), P()),
        out_specs=(P(("grp", "blk"), None, None), P(("grp", "blk"), None)),
        check_vma=False,
    )
```
